32 devices in a mesh: ctx: 8 (over z, y), head: 4 (over x, core).
Axes of the slice: x: 2, y: 2, z: 4, core: 2. Of those that a mesh axis runs over, the one named last changes fastest.
Arguments:
- queries: bfloat16 [2048, 4096], P('ctx', 'head'), may hold values from -10 to 10
- key_states: bfloat16 [2048, 256], P('ctx'), may hold values from -10 to 10
- value_states: bfloat16 [2048, 256], P('ctx'), may hold values from -6 to 6
- vertical_blocks: int32 [32, 4], P('head'), may hold values from 0 to 15, as said below
- slash_offsets: int32 [32, 4], P('head'), may hold values from 0 to 15, as said below
- positions: int32 [2048], P('ctx'), may hold values from 0 to 32767, as said below
- out_weight: bfloat16 [4096, 16384], P('head', 'ctx'), may hold values from -0.5 to 0.5
Outputs:
- projected: bfloat16 [2048, 16384], P('head', 'ctx')
The draws below stay inside these ranges and needn't reach their ends.
Inputs may be any that keep to these rules, and one draw needn't show every extreme that they name: `vertical_blocks`: each head's 4 vertical blocks are distinct. `slash_offsets`: each head's 4 offsets are distinct and the first of them is 0. `positions`: positions rise by one inside each block of 128 tokens; block b starts at a multiple of 128 at or after b * 2048 and before (b + 1) * 2048.
All inputs are finite; a program needn't handle non-finite values.
Results may differ from the reference program's by a relative error of at most 0.025.
Values may be sent and summed in bfloat16 or wider, within the bound.
No kernel may reach another device: no remote copies, remote signals or barrier semaphores. Data moves between devices by JAX's collectives and lax.ppermute only.
A program may use at most 64 MiB of HBM per device.

```python
import math
import jax
import jax.numpy as jnp
from jax import lax

D = 16384
HD = 128
GROUP = 16
BLK = 128
NV = 4
NS = 4
PROMPT = 32768
HEADS = 32
KV_HEADS = 2
TOKENS = 2048
NB = 16
N_HEAD = 4


def draw_queries(key, part):
    noise_key = jax.random.fold_in(key, 1)
    base = jnp.clip(2.0 * jax.random.normal(noise_key, (TOKENS, HEADS, HD), jnp.float32), -10.0, 10.0)
    return base.reshape(TOKENS, HEADS * HD).astype(jnp.bfloat16)


def draw_key_states(key, part):
    noise_key = jax.random.fold_in(key, 2)
    base = jnp.clip(jax.random.normal(noise_key, (TOKENS, KV_HEADS, HD), jnp.float32), -6.0, 6.0)
    return base.reshape(TOKENS, KV_HEADS * HD).astype(jnp.bfloat16)


def block_order(one_key):
    return jax.random.permutation(one_key, NB)


def offset_order(one_key):
    return jax.random.permutation(one_key, NB - 1)


def draw_vertical_blocks(key, part):
    head_keys = jax.random.split(jax.random.fold_in(key, 3), HEADS)
    orders = jax.vmap(block_order)(head_keys)
    return orders[:, :NV].astype(jnp.int32)


def draw_slash_offsets(key, part):
    head_keys = jax.random.split(jax.random.fold_in(key, 4), HEADS)
    orders = jax.vmap(offset_order)(head_keys)[:, :NS - 1] + 1
    leading = jnp.zeros((HEADS, 1), jnp.int32)
    return jnp.concatenate([leading, orders.astype(jnp.int32)], axis=1)


def draw_positions(key, part):
    stride = PROMPT // NB
    offsets = jax.random.randint(jax.random.fold_in(key, 5), (NB,), 0, stride // BLK) * BLK
    starts = jnp.arange(NB, dtype=jnp.int32) * stride + offsets
    return (jnp.repeat(starts, BLK) + jnp.tile(jnp.arange(BLK, dtype=jnp.int32), NB)).astype(jnp.int32)


def steps_of(stream_key, extent, cuts, low, high):
    loudness, own = 1.0, jax.random.fold_in(stream_key, 6)
    for position, shards_of in cuts:
        heights = jnp.exp(jax.random.uniform(jax.random.fold_in(own, position), (shards_of,), jnp.float32, low / len(cuts), high / len(cuts)))
        loudness = loudness * jnp.repeat(heights, extent[position] // shards_of).reshape([-1 if axis == position else 1 for axis in range(len(extent))])
    return loudness


def scatter_about(key, shape, scale, reach, shards=(), kind=jnp.bfloat16):
    drawn = jax.random.normal(key, shape, jnp.float32) * scale
    if len(shards) > 0:
        drawn = steps_of(key, shape, shards, -0.22, 0.18) * drawn
    return jnp.clip(drawn, min=-reach, max=reach).astype(kind)


def setup_inputs(seed: int = 0) -> dict:
    arg_keys = jax.random.split(jax.random.key(seed), 8)
    return {
        "queries": draw_queries(jax.random.fold_in(arg_keys[7], 71), 0),
        "key_states": draw_key_states(jax.random.fold_in(arg_keys[7], 71), 0),
        "value_states": scatter_about(arg_keys[2], (TOKENS, KV_HEADS * HD), 1.0, 6.0, ((0, 8),)),
        "vertical_blocks": draw_vertical_blocks(jax.random.fold_in(arg_keys[7], 71), 0),
        "slash_offsets": draw_slash_offsets(jax.random.fold_in(arg_keys[7], 71), 0),
        "positions": draw_positions(jax.random.fold_in(arg_keys[7], 71), 0),
        "out_weight": scatter_about(arg_keys[6], (HEADS * HD, D), (HEADS * HD // 32) ** -0.5, 0.5, ((0, 4), (1, 8))),
    }


def rotate_heads(states, positions):
    half_width = states.shape[-1] // 2
    exponents = jnp.arange(half_width, dtype=jnp.float32) * (2.0 / states.shape[-1])
    inverse_freq = 500000.0 ** (-exponents)
    angles = positions.astype(jnp.float32)[:, None] * inverse_freq[None, :]
    cosine = jnp.cos(angles)[:, None, :]
    sine_part = jnp.sin(angles)[:, None, :]
    front_half = states[..., :half_width]
    back_half = states[..., half_width:]
    return jnp.concatenate([front_half * cosine - back_half * sine_part, back_half * cosine + front_half * sine_part], axis=-1)

def reference(queries, key_states, value_states, vertical_blocks, slash_offsets, positions, out_weight):
    query_rot = rotate_heads(queries.astype(jnp.float32).reshape(TOKENS, HEADS, HD), positions).astype(jnp.bfloat16)
    key_rot = rotate_heads(key_states.astype(jnp.float32).reshape(TOKENS, KV_HEADS, HD), positions).astype(jnp.bfloat16)
    value_heads = value_states.reshape(TOKENS, KV_HEADS, HD)
    block_index = jnp.arange(NB, dtype=jnp.int32)
    token_block = jnp.arange(TOKENS, dtype=jnp.int32) // BLK
    causal_pairs = jnp.arange(TOKENS)[None, :] <= jnp.arange(TOKENS)[:, None]

    def one_head(head):
        group_id = head // GROUP
        vertical_row = lax.dynamic_index_in_dim(vertical_blocks, head, 0, keepdims=False)
        slash_row = lax.dynamic_index_in_dim(slash_offsets, head, 0, keepdims=False)
        later = block_index[:, None]
        earlier = block_index[None, :]
        in_vertical = jnp.any(earlier[..., None] == vertical_row[None, None, :], axis=-1)
        in_slash = jnp.any((later - earlier)[..., None] == slash_row[None, None, :], axis=-1)
        block_mask = (earlier <= later) & (in_vertical | in_slash)
        token_mask = block_mask[token_block][:, token_block] & causal_pairs
        query_head = lax.dynamic_index_in_dim(query_rot, head, 1, keepdims=False)
        key_head = lax.dynamic_index_in_dim(key_rot, group_id, 1, keepdims=False)
        value_head = lax.dynamic_index_in_dim(value_heads, group_id, 1, keepdims=False)
        scores = jnp.dot(query_head, key_head.T, preferred_element_type=jnp.float32) / math.sqrt(HD)
        masked = jnp.where(token_mask, scores, -1e+30)
        row_max = lax.optimization_barrier(jnp.max(masked, axis=1, keepdims=True))
        exponentials = jnp.exp(masked - row_max)
        weights = (exponentials / lax.optimization_barrier(jnp.sum(exponentials, axis=1, keepdims=True))).astype(jnp.bfloat16)
        return jnp.dot(weights, value_head, preferred_element_type=jnp.float32).astype(jnp.bfloat16)
    per_head = lax.map(one_head, jnp.arange(HEADS, dtype=jnp.int32))
    head_out = jnp.transpose(per_head, (1, 0, 2)).reshape(TOKENS, HEADS * HD)
    group_rows = HEADS * HD // N_HEAD
    accumulated = jnp.zeros((TOKENS, D), jnp.float32)
    for group_id in range(N_HEAD):
        partial_value = jnp.dot(head_out[:, group_id * group_rows:(group_id + 1) * group_rows], out_weight[group_id * group_rows:(group_id + 1) * group_rows], preferred_element_type=jnp.float32).astype(jnp.bfloat16)
        partial_value = lax.optimization_barrier(partial_value)
        accumulated = accumulated + partial_value.astype(jnp.float32)
    return accumulated.astype(jnp.bfloat16)
```

```python
import functools
import math

import jax
import jax.numpy as jnp
from jax import lax
from jax.experimental import pallas as pl
from jax.experimental.pallas import tpu as pltpu
from jax.sharding import PartitionSpec as P

HD = 128
GROUP = 16
BLK = 128
NEG = -1e30
SCALE = math.log2(math.e) / math.sqrt(HD)


def rotation_tables(positions):
    half = HD // 2
    exponents = jnp.arange(half, dtype=jnp.float32) * (2.0 / HD)
    inverse_freq = 500000.0 ** (-exponents)
    angles = positions.astype(jnp.float32)[:, None] * inverse_freq[None, :]
    cosine, sine = jnp.cos(angles), jnp.sin(angles)
    return jnp.concatenate([cosine, cosine], axis=1), jnp.concatenate([-sine, sine], axis=1)


def rotate(states, cosine, sine):
    states = states.astype(jnp.float32)
    return states * cosine + pltpu.roll(states, HD // 2, 1) * sine


def key_kernel(place, keys, values, cosine, sine, out):
    first = pl.multiple_of(place[0] * BLK, BLK)
    lane = pl.multiple_of(place[1] * HD, HD)
    rows = pl.ds(first, BLK)
    rotated = rotate(keys[rows, pl.ds(lane, HD)], cosine[rows, :], sine[rows, :])
    out[:, :HD] = rotated.astype(out.dtype)
    out[:, HD:] = values[rows, pl.ds(lane, HD)]


def attention_kernel(place, vertical, slash, queries, cosine, sine, own, other, out):
    head = pl.program_id(0)
    ctx, core = place[0], place[1]
    tri = (
        lax.broadcasted_iota(jnp.int32, (BLK, BLK), 1)
        <= lax.broadcasted_iota(jnp.int32, (BLK, BLK), 0)
    )
    verts = [vertical[head, i] for i in range(vertical.shape[1])]
    query_blocks = queries.shape[0] // BLK
    for local in range(query_blocks):
        block = ctx * query_blocks + local
        rows = pl.ds(local * BLK, BLK)
        rot = rotate(queries[rows, :], cosine[rows, :], sine[rows, :]).astype(jnp.bfloat16)
        slots = [(block, None)]
        for v in verts:
            slots.append((v, v < block))
        for j in range(1, slash.shape[1]):
            u = block - slash[head, j]
            ok = u >= 0
            for v in verts:
                ok = jnp.logical_and(ok, u != v)
            slots.append((jnp.maximum(u, 0), ok))
        tiles, scores = [], []
        for u, ok in slots:
            start = pl.multiple_of(((u // 2) ^ ctx) * BLK, BLK)
            mine = (u % 2) == core
            tile = jnp.where(mine, own[pl.ds(start, BLK), :], other[pl.ds(start, BLK), :])
            s = lax.dot_general(
                rot, tile[:, :HD], (((1,), (1,)), ((), ())), preferred_element_type=jnp.float32
            )
            s = jnp.where(tri, s, NEG) if ok is None else s + jnp.where(ok, 0.0, NEG)
            tiles.append(tile)
            scores.append(s)
        top = functools.reduce(jnp.maximum, scores)
        top = jnp.max(top, axis=1, keepdims=True)
        total, acc = None, None
        for s, tile in zip(scores, tiles):
            e = jnp.exp2((s - top) * SCALE)
            total = e if total is None else total + e
            o = jnp.dot(e.astype(jnp.bfloat16), tile[:, HD:], preferred_element_type=jnp.float32)
            acc = o if acc is None else acc + o
        total = jnp.sum(total, axis=1, keepdims=True)
        out[rows, :] = (acc / total).astype(out.dtype)


def attend(ctx, core, vertical, slash, queries, cosine, sine, own, other):
    tokens, width = queries.shape
    heads = width // HD
    whole = lambda a: pl.BlockSpec(a.shape, lambda h, *_: (0, 0))
    return pl.pallas_call(
        attention_kernel,
        grid_spec=pltpu.PrefetchScalarGridSpec(
            num_scalar_prefetch=3,
            grid=(heads,),
            in_specs=[
                pl.BlockSpec((tokens, HD), lambda h, *_: (0, h)),
                whole(cosine),
                whole(sine),
                whole(own),
                whole(other),
            ],
            out_specs=pl.BlockSpec((tokens, HD), lambda h, *_: (0, h)),
        ),
        out_shape=jax.ShapeDtypeStruct((tokens, width), jnp.bfloat16),
        name="attention",
    )(jnp.stack([ctx, core]), vertical, slash, queries, cosine, sine, own, other)


def pack_keys(core, shared_head, key_states, value_states, cosine, sine):
    vmem = pl.BlockSpec(memory_space=pltpu.VMEM)
    return pl.pallas_call(
        key_kernel,
        in_specs=[pl.BlockSpec(memory_space=pltpu.SMEM)] + [vmem] * 4,
        out_specs=vmem,
        out_shape=jax.ShapeDtypeStruct((BLK, 2 * HD), jnp.bfloat16),
        name="pack_keys",
    )(jnp.stack([core, shared_head]), key_states, value_states, cosine, sine)


def route(table):
    pairs = []
    for y in range(2):
        for x in range(2):
            for (z, c), (z2, c2) in table.items():
                if x == 1:
                    z, c, z2, c2 = 3 - z, 1 - c, 3 - z2, 1 - c2
                pairs.append((((z * 2 + y) * 2 + x) * 2 + c, ((z2 * 2 + y) * 2 + x) * 2 + c2))
    return sorted(pairs)


HOP_1 = {(2, 0): (1, 0), (3, 1): (2, 1), (0, 0): (2, 0), (1, 1): (0, 1)}
HOP_2 = {(3, 1): (1, 1), (2, 0): (3, 0), (1, 1): (2, 1), (0, 0): (1, 0)}
HOP_3 = {(1, 0): (0, 0), (1, 1): (0, 1), (2, 0): (3, 0), (2, 1): (3, 1)}


def routed(head_out, out_weight, ctx_index, head_index):
    both = ("ctx", "head")
    z, y, x, core = ctx_index // 2, ctx_index % 2, head_index // 2, head_index % 2
    far = jnp.where(x == 0, z, 3 - z)
    lane = jnp.where(x == 0, core, 1 - core)
    swap_core = [(i, i ^ 1) for i in range(4)]
    swap_x = [(i, i ^ 2) for i in range(4)]
    swap_y = [(i, i ^ 1) for i in range(8)]
    weight = jnp.concatenate([out_weight, lax.ppermute(out_weight, "head", swap_core)], axis=0)
    block = jnp.concatenate([head_out, lax.ppermute(head_out, "head", swap_core)], axis=1)
    hop_1 = lax.ppermute(block, both, route(HOP_1))
    hop_2 = lax.ppermute(block, both, route(HOP_2))
    inner = jnp.where(lane == 0, hop_1, hop_2)
    hop_3 = lax.ppermute(inner, both, route(HOP_3))
    early = jnp.where(z % 2 == core, block, jnp.where(far % 2 == 0, hop_1, hop_2))
    late = jnp.where((far == 1) | (far == 2), inner, hop_3)
    first = far >= 2
    sent = jnp.where(first, early, late)
    kept = jnp.where(first, late, early)
    sent_y = lax.ppermute(sent, "ctx", swap_y)
    kept_y = lax.ppermute(kept, "ctx", swap_y)

    def project(rows):
        return jnp.dot(rows, weight, preferred_element_type=jnp.float32)

    come = lax.ppermute(project(sent).astype(jnp.bfloat16), "head", swap_x)
    come_y = lax.ppermute(project(sent_y).astype(jnp.bfloat16), "head", swap_x)
    rows = block.shape[0]
    own = (project(kept) + come.astype(jnp.float32)).astype(jnp.bfloat16)
    own_y = (project(kept_y) + come_y.astype(jnp.float32)).astype(jnp.bfloat16)
    out = jnp.zeros((2 * rows, out_weight.shape[1]), jnp.bfloat16)
    out = lax.dynamic_update_slice(out, own, (y * rows, 0))
    return lax.dynamic_update_slice(out, own_y, ((1 - y) * rows, 0))


def collected(head_out, out_weight):
    rows = lax.all_gather(head_out, "ctx", axis=0, tiled=True)
    partial_terms = jnp.dot(rows, out_weight, preferred_element_type=jnp.float32)
    return lax.psum_scatter(
        partial_terms.astype(jnp.bfloat16), "head", scatter_dimension=0, tiled=True
    )


def per_device(
    ctx_size,
    head_size,
    queries,
    key_states,
    value_states,
    vertical_blocks,
    slash_offsets,
    positions,
    out_weight,
):
    local_heads = queries.shape[1] // HD
    head_index = lax.axis_index("head")
    ctx_index = lax.axis_index("ctx")
    core = head_index % 2
    shared_head = head_index * local_heads // GROUP
    cosine, sine = rotation_tables(positions)
    piece = pack_keys(core, shared_head, key_states, value_states, cosine, sine)
    pieces = [piece] + [
        lax.ppermute(piece, "ctx", [(i, i ^ d) for i in range(ctx_size)])
        for d in range(1, ctx_size)
    ]
    own = jnp.concatenate(pieces, axis=0)
    other = lax.ppermute(own, "head", [(i, i ^ 1) for i in range(head_size)])
    head_out = attend(
        ctx_index, core, vertical_blocks, slash_offsets, queries, cosine, sine, own, other
    )
    if (ctx_size, head_size) == (8, 4):
        return routed(head_out, out_weight, ctx_index, head_index)
    return collected(head_out, out_weight)


def solution(mesh):
    placed = (
        P("ctx", "head"),
        P("ctx", None),
        P("ctx", None),
        P("head", None),
        P("head", None),
        P("ctx"),
        P("head", "ctx"),
    )
    return jax.shard_map(
        functools.partial(per_device, mesh.shape["ctx"], mesh.shape["head"]),
        mesh=mesh,
        in_specs=placed,
        out_specs=P("head", "ctx"),
        check_vma=False,
    )
```

```python
import functools
import math

import jax
import jax.numpy as jnp
from jax import lax
from jax.experimental import pallas as pl
from jax.experimental.pallas import tpu as pltpu
from jax.sharding import PartitionSpec as P

HD = 128
GROUP = 16
BLK = 128
NEG = -1e30
GRANT = 20 << 20
SCALE = math.log2(math.e) / math.sqrt(HD)
VMEM = pl.BlockSpec(memory_space=pltpu.VMEM)
SMEM = pl.BlockSpec(memory_space=pltpu.SMEM)


def rotation_tables(positions):
    half = HD // 2
    exponents = jnp.arange(half, dtype=jnp.float32) * (2.0 / HD)
    inverse_freq = 500000.0 ** (-exponents)
    angles = positions.astype(jnp.float32)[:, None] * inverse_freq[None, :]
    cosine, sine = jnp.cos(angles), jnp.sin(angles)
    return jnp.concatenate([cosine, cosine], axis=1), jnp.concatenate([-sine, sine], axis=1)


def rotate(states, cosine, sine):
    states = states.astype(jnp.float32)
    rotated = states * cosine + pltpu.roll(states, HD // 2, 1) * sine
    return rotated.astype(jnp.bfloat16)


def pack_kernel(place, keys, values, cosine, sine, piece):
    rows = pl.ds(pl.multiple_of(place[0] * BLK, BLK), BLK)
    lane = pl.ds(pl.multiple_of(place[1] * HD, HD), HD)
    piece[:, :HD] = rotate(keys[rows, lane], cosine[rows, :], sine[rows, :])
    piece[:, HD:] = values[rows, lane]


def pack(place, key_states, value_states, cosine, sine):
    return pl.pallas_call(
        pack_kernel,
        in_specs=[SMEM] + [VMEM] * 4,
        out_specs=VMEM,
        out_shape=jax.ShapeDtypeStruct((BLK, 2 * HD), jnp.bfloat16),
        compiler_params=pltpu.CompilerParams(vmem_limit_bytes=GRANT),
        name="pack",
    )(place, key_states, value_states, cosine, sine)


def turn_kernel(queries, cosine, sine, out):
    for head in range(queries.shape[1] // HD):
        part = (slice(None), slice(head * HD, (head + 1) * HD))
        out[part] = rotate(queries[part], cosine[...], sine[...])


def turn(queries, cosine, sine):
    return pl.pallas_call(
        turn_kernel,
        in_specs=[VMEM] * 3,
        out_specs=VMEM,
        out_shape=jax.ShapeDtypeStruct(queries.shape, jnp.bfloat16),
        compiler_params=pltpu.CompilerParams(vmem_limit_bytes=GRANT),
        name="turn",
    )(queries, cosine, sine)


def attended(table, head, verticals, slashes, block, rot, keys, values, causal):
    at = head * (verticals + slashes)
    verts = [table[at + i] for i in range(verticals)]
    slots = [(block, None)] + [(v, v < block) for v in verts]
    for j in range(1, slashes):
        u = block - table[at + verticals + j]
        valid = u >= 0
        for v in verts:
            valid = jnp.logical_and(valid, u != v)
        slots.append((jnp.maximum(u, 0), valid))
    rows = [pl.ds(pl.multiple_of(u * BLK, BLK), BLK) for u, _ in slots]
    pairs = [slice(i, i + 2) for i in range(0, len(slots), 2)]
    scores = []
    for pair in pairs:
        tile = jnp.concatenate([keys[r, :] for r in rows[pair]], axis=0)
        both = lax.dot_general(
            rot, tile, (((1,), (1,)), ((), ())), preferred_element_type=jnp.float32
        )
        for i, (_, valid) in enumerate(slots[pair]):
            s = both[:, i * BLK : (i + 1) * BLK]
            scores.append(
                jnp.where(causal, s, NEG) if valid is None else s + jnp.where(valid, 0.0, NEG)
            )
    top = jnp.max(functools.reduce(jnp.maximum, scores), axis=1, keepdims=True)
    weights = [jnp.exp2((s - top) * SCALE).astype(jnp.bfloat16) for s in scores]
    total = None
    for pair in pairs:
        tile = jnp.concatenate([values[r, :] for r in rows[pair]], axis=0)
        part = jnp.dot(
            jnp.concatenate(weights[pair], axis=1), tile, preferred_element_type=jnp.float32
        )
        total = part if total is None else total + part
    return (total[:, :HD] / total[:, HD:]).astype(jnp.bfloat16)


def attention_kernel(shape, table, queries, own, other, *refs):
    verticals, slashes, at, step = shape
    *outs, keys, values = refs
    ctx, core = table[at], table[at + 1]

    @pl.when(pl.program_id(0) == 0)
    def _():
        for d in range(own.shape[0] // BLK):
            for ref, parity in ((own, core), (other, 1 - core)):
                rows = pl.ds(pl.multiple_of(((ctx ^ d) * 2 + parity) * BLK, BLK), BLK)
                keys[rows, :] = ref[d * BLK : (d + 1) * BLK, :HD]
                values[rows, :HD] = ref[d * BLK : (d + 1) * BLK, HD:]
        values[:, HD:] = jnp.ones((values.shape[0], HD), values.dtype)

    causal = lax.broadcasted_iota(jnp.int32, (BLK, BLK), 1) <= lax.broadcasted_iota(
        jnp.int32, (BLK, BLK), 0
    )
    for i in range(step):
        head = pl.program_id(0) * step + i
        lanes = slice(i * HD, (i + 1) * HD)
        for local, out in enumerate(outs):
            rot = queries[local * BLK : (local + 1) * BLK, lanes]
            index = ctx * len(outs) + local
            out[:, lanes] = attended(
                table, head, verticals, slashes, index, rot, keys, values, causal
            )


def attend(table, at, verticals, slashes, queries, own, other):
    tokens, width = queries.shape
    step = 4
    whole = lambda a: pl.BlockSpec(a.shape, lambda h, _: (0, 0))
    part = lambda rows: pl.BlockSpec((rows, step * HD), lambda h, _: (0, h))
    blocks = tokens // BLK
    keys = 2 * own.shape[0]
    return pl.pallas_call(
        functools.partial(attention_kernel, (verticals, slashes, at, step)),
        grid_spec=pltpu.PrefetchScalarGridSpec(
            num_scalar_prefetch=1,
            grid=(width // (step * HD),),
            in_specs=[part(tokens), whole(own), whole(other)],
            out_specs=[part(BLK)] * blocks,
            scratch_shapes=[
                pltpu.VMEM((keys, HD), jnp.bfloat16),
                pltpu.VMEM((keys, 2 * HD), jnp.bfloat16),
            ],
        ),
        out_shape=[jax.ShapeDtypeStruct((BLK, width), jnp.bfloat16)] * blocks,
        compiler_params=pltpu.CompilerParams(vmem_limit_bytes=GRANT),
        name="attention",
    )(table, queries, own, other)


def project_kernel(rows, own, other, out):
    depth, tile = own.shape[0], 512
    first, second = rows[:, :depth], rows[:, depth:]
    for j in range(0, own.shape[1], tile):
        part = slice(j, j + tile)
        total = jnp.dot(first, own[:, part], preferred_element_type=jnp.float32)
        total += jnp.dot(second, other[:, part], preferred_element_type=jnp.float32)
        out[:, part] = total.astype(out.dtype)


def project(rows, own, other, kind):
    count, depth = rows.shape
    width = own.shape[1]
    return pl.pallas_call(
        project_kernel,
        in_specs=[VMEM] * 3,
        out_specs=VMEM,
        out_shape=jax.ShapeDtypeStruct((count, width), kind),
        compiler_params=pltpu.CompilerParams(vmem_limit_bytes=GRANT),
        cost_estimate=pl.CostEstimate(
            flops=2 * count * depth * width,
            bytes_accessed=2 * (count * depth + count * width),
            transcendentals=0,
        ),
        name="project",
    )(rows, own, other)


def route(table):
    pairs = []
    for y in range(2):
        for x in range(2):
            for (z, c), (z2, c2) in table.items():
                if x == 1:
                    z, c, z2, c2 = 3 - z, 1 - c, 3 - z2, 1 - c2
                pairs.append((((z * 2 + y) * 2 + x) * 2 + c, ((z2 * 2 + y) * 2 + x) * 2 + c2))
    return sorted(pairs)


HOP_1 = {(2, 0): (1, 0), (3, 1): (2, 1), (0, 0): (2, 0), (1, 1): (0, 1)}
HOP_2 = {(3, 1): (1, 1), (2, 0): (3, 0), (1, 1): (2, 1), (0, 0): (1, 0)}
HOP_3 = {(1, 0): (0, 0), (1, 1): (0, 1), (2, 0): (3, 0), (2, 1): (3, 1)}


def routed(halves, out_weight, ctx_index, head_index):
    both = ("ctx", "head")
    z, y, x, core = ctx_index // 2, ctx_index % 2, head_index // 2, head_index % 2
    far = jnp.where(x == 0, z, 3 - z)
    lane = jnp.where(x == 0, core, 1 - core)
    swap_core = [(i, i ^ 1) for i in range(4)]
    swap_x = [(i, i ^ 2) for i in range(4)]
    swap_y = [(i, i ^ 1) for i in range(8)]
    weights = [
        pltpu.with_memory_space_constraint(w, pltpu.VMEM)
        for w in (out_weight, lax.ppermute(out_weight, "head", swap_core))
    ]
    home, inner, first = z % 2 == core, (far == 1) | (far == 2), far >= 2

    sent, kept = [], []
    for half in halves:
        block = jnp.concatenate([half, lax.ppermute(half, "head", swap_core)], axis=1)
        hop_1 = lax.ppermute(block, both, route(HOP_1))
        hop_2 = lax.ppermute(block, both, route(HOP_2))
        passed = jnp.where(lane == 0, hop_1, hop_2)
        hop_3 = lax.ppermute(passed, both, route(HOP_3))
        early = jnp.where(home, block, jnp.where(lane == 0, hop_2, hop_1))
        late = jnp.where(inner, passed, hop_3)
        sent.append(jnp.where(first, early, late))
        kept.append(jnp.where(first, late, early))
    sent += [lax.ppermute(rows, "ctx", swap_y) for rows in sent]
    kept += [lax.ppermute(rows, "ctx", swap_y) for rows in kept]
    parts = [project(rows, *weights, jnp.bfloat16) for rows in sent]
    come = [lax.ppermute(part, "head", swap_x) for part in parts]
    kept, parts = lax.optimization_barrier((kept, parts))
    own = [project(rows, *weights, jnp.float32) for rows in kept]
    rows = BLK * len(halves)
    out = jnp.zeros((2 * rows, out_weight.shape[1]), jnp.bfloat16)
    for i, (mine, theirs) in enumerate(zip(own, come)):
        total = (mine + theirs.astype(jnp.float32)).astype(jnp.bfloat16)
        local, other_y = i % len(halves), i // len(halves)
        at = jnp.where(other_y == 0, y, 1 - y) * rows + local * BLK
        out = lax.dynamic_update_slice(out, total, (at, 0))
    return out


def collected(head_out, out_weight):
    rows = lax.all_gather(head_out, "ctx", axis=0, tiled=True)
    partial_terms = jnp.dot(rows, out_weight, preferred_element_type=jnp.float32)
    return lax.psum_scatter(
        partial_terms.astype(jnp.bfloat16), "head", scatter_dimension=0, tiled=True
    )


def per_device(
    ctx_size,
    head_size,
    queries,
    key_states,
    value_states,
    vertical_blocks,
    slash_offsets,
    positions,
    out_weight,
):
    local_heads = queries.shape[1] // HD
    head_index = lax.axis_index("head")
    ctx_index = lax.axis_index("ctx")
    core = head_index % 2
    shared_head = head_index * local_heads // GROUP
    counts = (vertical_blocks.shape[1], slash_offsets.shape[1])
    swap_core = [(i, i ^ 1) for i in range(head_size)]
    table = jnp.concatenate([vertical_blocks, slash_offsets], axis=1).reshape(-1)
    at = table.shape[0]
    table = jnp.concatenate([table, jnp.stack([ctx_index, core])])
    cosine, sine = rotation_tables(positions)
    piece = pack(jnp.stack([core, shared_head]), key_states, value_states, cosine, sine)
    pieces = [piece] + [
        lax.ppermute(piece, "ctx", [(i, i ^ d) for i in range(ctx_size)])
        for d in range(1, ctx_size)
    ]
    rotated = turn(queries, cosine, sine)
    own, rotated, table = lax.optimization_barrier(
        (jnp.concatenate(pieces, axis=0), rotated, table)
    )
    other = lax.ppermute(own, "head", swap_core)
    halves = attend(table, at, *counts, rotated, own, other)
    if (ctx_size, head_size) == (8, 4):
        return routed(halves, out_weight, ctx_index, head_index)
    return collected(jnp.concatenate(halves, axis=0), out_weight)


def solution(mesh):
    placed = (
        P("ctx", "head"),
        P("ctx", None),
        P("ctx", None),
        P("head", None),
        P("head", None),
        P("ctx"),
        P("head", "ctx"),
    )
    return jax.shard_map(
        functools.partial(per_device, mesh.shape["ctx"], mesh.shape["head"]),
        mesh=mesh,
        in_specs=placed,
        out_specs=P("head", "ctx"),
        check_vma=False,
    )
```

```python
import functools
import math

import jax
import jax.numpy as jnp
from jax import lax
from jax.experimental import pallas as pl
from jax.experimental.pallas import tpu as pltpu
from jax.sharding import PartitionSpec as P

HD = 128
GROUP = 16
BLK = 128
NEG = -1e30
GRANT = 20 << 20
SCALE = math.log2(math.e) / math.sqrt(HD)
VMEM = pl.BlockSpec(memory_space=pltpu.VMEM)
SMEM = pl.BlockSpec(memory_space=pltpu.SMEM)


def rotation_tables(positions):
    half = HD // 2
    exponents = jnp.arange(half, dtype=jnp.float32) * (2.0 / HD)
    inverse_freq = 500000.0 ** (-exponents)
    angles = positions.astype(jnp.float32)[:, None] * inverse_freq[None, :]
    cosine, sine = jnp.cos(angles), jnp.sin(angles)
    return jnp.concatenate([cosine, cosine], axis=1), jnp.concatenate([-sine, sine], axis=1)


def rotate(states, cosine, sine):
    states = states.astype(jnp.float32)
    rotated = states * cosine + pltpu.roll(states, HD // 2, 1) * sine
    return rotated.astype(jnp.bfloat16)


def pack_kernel(place, keys, values, cosine, sine, piece):
    rows = pl.ds(pl.multiple_of(place[0] * BLK, BLK), BLK)
    lane = pl.ds(pl.multiple_of(place[1] * HD, HD), HD)
    piece[:, :HD] = rotate(keys[rows, lane], cosine[rows, :], sine[rows, :])
    piece[:, HD:] = values[rows, lane]


def pack(place, key_states, value_states, cosine, sine):
    return pl.pallas_call(
        pack_kernel,
        in_specs=[SMEM] + [VMEM] * 4,
        out_specs=VMEM,
        out_shape=jax.ShapeDtypeStruct((BLK, 2 * HD), jnp.bfloat16),
        compiler_params=pltpu.CompilerParams(vmem_limit_bytes=GRANT),
        name="pack",
    )(place, key_states, value_states, cosine, sine)


def turn_kernel(queries, cosine, sine, out):
    for head in range(queries.shape[1] // HD):
        part = (slice(None), slice(head * HD, (head + 1) * HD))
        out[part] = rotate(queries[part], cosine[...], sine[...])


def turn(queries, cosine, sine):
    return pl.pallas_call(
        turn_kernel,
        in_specs=[VMEM] * 3,
        out_specs=VMEM,
        out_shape=jax.ShapeDtypeStruct(queries.shape, jnp.bfloat16),
        compiler_params=pltpu.CompilerParams(vmem_limit_bytes=GRANT),
        name="turn",
    )(queries, cosine, sine)


def attended(table, head, verticals, slashes, block, rot, keys, values, causal):
    at = head * (verticals + slashes)
    verts = [table[at + i] for i in range(verticals)]
    slots = [(block, None)] + [(v, v < block) for v in verts]
    for j in range(1, slashes):
        u = block - table[at + verticals + j]
        valid = u >= 0
        for v in verts:
            valid = jnp.logical_and(valid, u != v)
        slots.append((jnp.maximum(u, 0), valid))
    rows = [pl.ds(pl.multiple_of(u * BLK, BLK), BLK) for u, _ in slots]
    pairs = [slice(i, i + 2) for i in range(0, len(slots), 2)]
    scores = []
    for pair in pairs:
        tile = jnp.concatenate([keys[r, :] for r in rows[pair]], axis=0)
        both = lax.dot_general(
            rot, tile, (((1,), (1,)), ((), ())), preferred_element_type=jnp.float32
        )
        for i, (_, valid) in enumerate(slots[pair]):
            s = both[:, i * BLK : (i + 1) * BLK]
            scores.append(
                jnp.where(causal, s, NEG) if valid is None else s + jnp.where(valid, 0.0, NEG)
            )
    top = jnp.max(functools.reduce(jnp.maximum, scores), axis=1, keepdims=True)
    weights = [jnp.exp2((s - top) * SCALE).astype(jnp.bfloat16) for s in scores]
    total = None
    for pair in pairs:
        tile = jnp.concatenate([values[r, :] for r in rows[pair]], axis=0)
        part = jnp.dot(
            jnp.concatenate(weights[pair], axis=1), tile, preferred_element_type=jnp.float32
        )
        total = part if total is None else total + part
    return (total[:, :HD] / total[:, HD:]).astype(jnp.bfloat16)


def attention_kernel(shape, table, queries, own, other, *refs):
    verticals, slashes, at, step = shape
    *outs, keys, values = refs
    ctx, core = table[at], table[at + 1]

    @pl.when(pl.program_id(0) == 0)
    def _():
        for d in range(own.shape[0] // BLK):
            for ref, parity in ((own, core), (other, 1 - core)):
                rows = pl.ds(pl.multiple_of(((ctx ^ d) * 2 + parity) * BLK, BLK), BLK)
                keys[rows, :] = ref[d * BLK : (d + 1) * BLK, :HD]
                values[rows, :HD] = ref[d * BLK : (d + 1) * BLK, HD:]
        values[:, HD:] = jnp.ones((values.shape[0], HD), values.dtype)

    causal = lax.broadcasted_iota(jnp.int32, (BLK, BLK), 1) <= lax.broadcasted_iota(
        jnp.int32, (BLK, BLK), 0
    )
    for i in range(step):
        head = pl.program_id(0) * step + i
        lanes = slice(i * HD, (i + 1) * HD)
        for local, out in enumerate(outs):
            rot = queries[local * BLK : (local + 1) * BLK, lanes]
            index = ctx * len(outs) + local
            out[:, lanes] = attended(
                table, head, verticals, slashes, index, rot, keys, values, causal
            )


def attend(table, at, verticals, slashes, queries, own, other):
    tokens, width = queries.shape
    step = 4
    whole = lambda a: pl.BlockSpec(a.shape, lambda h, _: (0, 0))
    part = lambda rows: pl.BlockSpec((rows, step * HD), lambda h, _: (0, h))
    blocks = tokens // BLK
    keys = 2 * own.shape[0]
    return pl.pallas_call(
        functools.partial(attention_kernel, (verticals, slashes, at, step)),
        grid_spec=pltpu.PrefetchScalarGridSpec(
            num_scalar_prefetch=1,
            grid=(width // (step * HD),),
            in_specs=[part(tokens), whole(own), whole(other)],
            out_specs=[part(BLK)] * blocks,
            scratch_shapes=[
                pltpu.VMEM((keys, HD), jnp.bfloat16),
                pltpu.VMEM((keys, 2 * HD), jnp.bfloat16),
            ],
        ),
        out_shape=[jax.ShapeDtypeStruct((BLK, width), jnp.bfloat16)] * blocks,
        compiler_params=pltpu.CompilerParams(vmem_limit_bytes=GRANT),
        name="attention",
    )(table, queries, own, other)


def project_kernel(rows, own, other, out):
    depth, tile = own.shape[0], 512
    first, second = rows[:, :depth], rows[:, depth:]
    for j in range(0, own.shape[1], tile):
        part = slice(j, j + tile)
        total = jnp.dot(first, own[:, part], preferred_element_type=jnp.float32)
        total += jnp.dot(second, other[:, part], preferred_element_type=jnp.float32)
        out[:, part] = total.astype(out.dtype)


def project(rows, own, other, kind):
    count, depth = rows.shape
    width = own.shape[1]
    return pl.pallas_call(
        project_kernel,
        in_specs=[VMEM] * 3,
        out_specs=VMEM,
        out_shape=jax.ShapeDtypeStruct((count, width), kind),
        compiler_params=pltpu.CompilerParams(vmem_limit_bytes=GRANT),
        cost_estimate=pl.CostEstimate(
            flops=2 * count * depth * width,
            bytes_accessed=2 * (count * depth + count * width),
            transcendentals=0,
        ),
        name="project",
    )(rows, own, other)


def route(table):
    pairs = []
    for y in range(2):
        for x in range(2):
            for (z, c), (z2, c2) in table.items():
                if x == 1:
                    z, c, z2, c2 = 3 - z, 1 - c, 3 - z2, 1 - c2
                pairs.append((((z * 2 + y) * 2 + x) * 2 + c, ((z2 * 2 + y) * 2 + x) * 2 + c2))
    return sorted(pairs)


HOP_1 = {(2, 0): (1, 0), (3, 1): (2, 1), (0, 0): (2, 0), (1, 1): (0, 1)}
HOP_2 = {(3, 1): (1, 1), (2, 0): (3, 0), (1, 1): (2, 1), (0, 0): (1, 0)}
HOP_3 = {(1, 0): (0, 0), (1, 1): (0, 1), (2, 0): (3, 0), (2, 1): (3, 1)}


def routed(halves, out_weight, ctx_index, head_index):
    both = ("ctx", "head")
    z, y, x, core = ctx_index // 2, ctx_index % 2, head_index // 2, head_index % 2
    far = jnp.where(x == 0, z, 3 - z)
    lane = jnp.where(x == 0, core, 1 - core)
    swap_core = [(i, i ^ 1) for i in range(4)]
    swap_x = [(i, i ^ 2) for i in range(4)]
    swap_y = [(i, i ^ 1) for i in range(8)]
    weights = [
        pltpu.with_memory_space_constraint(w, pltpu.VMEM)
        for w in (out_weight, lax.ppermute(out_weight, "head", swap_core))
    ]
    home, inner, first = z % 2 == core, (far == 1) | (far == 2), far >= 2

    sent, kept, parts = [], [], []
    hops = []
    for half in halves:
        block = jnp.concatenate([half, lax.ppermute(half, "head", swap_core)], axis=1)
        hop_1 = lax.ppermute(block, both, route(HOP_1))
        hop_2 = lax.ppermute(block, both, route(HOP_2))
        hops.append((block, hop_1, hop_2))
    for block, hop_1, hop_2 in hops:
        passed = jnp.where(lane == 0, hop_1, hop_2)
        hop_3 = lax.ppermute(passed, both, route(HOP_3))
        if parts:
            hop_3, _ = lax.optimization_barrier((hop_3, parts[-1]))
        early = jnp.where(home, block, jnp.where(lane == 0, hop_2, hop_1))
        late = jnp.where(inner, passed, hop_3)
        sent.append(jnp.where(first, early, late))
        kept.append(jnp.where(first, late, early))
        parts.append(project(sent[-1], *weights, jnp.bfloat16))
    after = lambda rows, *others: lax.optimization_barrier((rows, others))[0]
    sent_y = [lax.ppermute(rows, "ctx", swap_y) for rows in sent]
    come = [lax.ppermute(part, "head", swap_x) for part in parts]
    for i, rows in enumerate(sent_y):
        parts.append(project(after(rows, come[i], parts[-1]), *weights, jnp.bfloat16))
        come.append(lax.ppermute(parts[-1], "head", swap_x))
    kept_y = [lax.ppermute(after(rows, parts[1]), "ctx", swap_y) for rows in kept]
    own = [project(after(jnp.concatenate(kept, axis=0), parts[3]), *weights, jnp.float32)]
    own.append(project(after(jnp.concatenate(kept_y, axis=0), own[0]), *weights, jnp.float32))
    own = [o[i * BLK : (i + 1) * BLK] for o in own for i in range(len(halves))]
    rows = BLK * len(halves)
    out = jnp.zeros((2 * rows, out_weight.shape[1]), jnp.bfloat16)
    for i, (mine, theirs) in enumerate(zip(own, come)):
        total = (mine + theirs.astype(jnp.float32)).astype(jnp.bfloat16)
        local, other_y = i % len(halves), i // len(halves)
        at = jnp.where(other_y == 0, y, 1 - y) * rows + local * BLK
        out = lax.dynamic_update_slice(out, total, (at, 0))
    return out


def collected(head_out, out_weight):
    rows = lax.all_gather(head_out, "ctx", axis=0, tiled=True)
    partial_terms = jnp.dot(rows, out_weight, preferred_element_type=jnp.float32)
    return lax.psum_scatter(
        partial_terms.astype(jnp.bfloat16), "head", scatter_dimension=0, tiled=True
    )


def per_device(
    ctx_size,
    head_size,
    queries,
    key_states,
    value_states,
    vertical_blocks,
    slash_offsets,
    positions,
    out_weight,
):
    local_heads = queries.shape[1] // HD
    head_index = lax.axis_index("head")
    ctx_index = lax.axis_index("ctx")
    core = head_index % 2
    shared_head = head_index * local_heads // GROUP
    counts = (vertical_blocks.shape[1], slash_offsets.shape[1])
    swap_core = [(i, i ^ 1) for i in range(head_size)]
    table = jnp.concatenate([vertical_blocks, slash_offsets], axis=1).reshape(-1)
    at = table.shape[0]
    table = jnp.concatenate([table, jnp.stack([ctx_index, core])])
    cosine, sine = rotation_tables(positions)
    piece = pack(jnp.stack([core, shared_head]), key_states, value_states, cosine, sine)
    pieces = [piece] + [
        lax.ppermute(piece, "ctx", [(i, i ^ d) for i in range(ctx_size)])
        for d in range(1, ctx_size)
    ]
    rotated = turn(queries, cosine, sine)
    own, rotated, table = lax.optimization_barrier(
        (jnp.concatenate(pieces, axis=0), rotated, table)
    )
    other = lax.ppermute(own, "head", swap_core)
    halves = attend(table, at, *counts, rotated, own, other)
    if (ctx_size, head_size) == (8, 4):
        return routed(halves, out_weight, ctx_index, head_index)
    return collected(jnp.concatenate(halves, axis=0), out_weight)


def solution(mesh):
    placed = (
        P("ctx", "head"),
        P("ctx", None),
        P("ctx", None),
        P("head", None),
        P("head", None),
        P("ctx"),
        P("head", "ctx"),
    )
    return jax.shard_map(
        functools.partial(per_device, mesh.shape["ctx"], mesh.shape["head"]),
        mesh=mesh,
        in_specs=placed,
        out_specs=P("head", "ctx"),
        check_vma=False,
    )
```

```python
import functools
import math

import jax
import jax.numpy as jnp
from jax import lax
from jax.experimental import pallas as pl
from jax.experimental.pallas import tpu as pltpu
from jax.sharding import PartitionSpec as P

HD = 128
GROUP = 16
BLK = 128
NEG = -1e30
GRANT = 20 << 20
BEFORE = {'hop_3_out_1': ('part_0',),
 'kept_out_0': ('part_1',),
 'kept_out_1': ('part_1',),
 'own_0': ('part_3',),
 'own_1': ('own_done_0',),
 'sent_2': ('come_0', 'part_1'),
 'sent_3': ('come_1', 'part_2'),
 'sent_out_1': ('sent_y_0',)}
SCALE = math.log2(math.e) / math.sqrt(HD)
VMEM = pl.BlockSpec(memory_space=pltpu.VMEM)
SMEM = pl.BlockSpec(memory_space=pltpu.SMEM)


class Ordered:
    def __init__(self):
        self.made = {}

    def put(self, name, value):
        self.made[name] = value
        return value

    def get(self, name, value):
        others = [self.made[other] for other in BEFORE.get(name, ()) if other in self.made]
        return lax.optimization_barrier((value, others))[0] if others else value


def rotation_tables(positions):
    half = HD // 2
    exponents = jnp.arange(half, dtype=jnp.float32) * (2.0 / HD)
    inverse_freq = 500000.0 ** (-exponents)
    angles = positions.astype(jnp.float32)[:, None] * inverse_freq[None, :]
    cosine, sine = jnp.cos(angles), jnp.sin(angles)
    return jnp.concatenate([cosine, cosine], axis=1), jnp.concatenate([-sine, sine], axis=1)


def rotate(states, cosine, sine):
    states = states.astype(jnp.float32)
    rotated = states * cosine + pltpu.roll(states, HD // 2, 1) * sine
    return rotated.astype(jnp.bfloat16)


def pack_kernel(place, keys, values, cosine, sine, piece):
    rows = pl.ds(pl.multiple_of(place[0] * BLK, BLK), BLK)
    lane = pl.ds(pl.multiple_of(place[1] * HD, HD), HD)
    piece[:, :HD] = rotate(keys[rows, lane], cosine[rows, :], sine[rows, :])
    piece[:, HD:] = values[rows, lane]


def pack(place, key_states, value_states, cosine, sine):
    return pl.pallas_call(
        pack_kernel,
        in_specs=[SMEM] + [VMEM] * 4,
        out_specs=VMEM,
        out_shape=jax.ShapeDtypeStruct((BLK, 2 * HD), jnp.bfloat16),
        compiler_params=pltpu.CompilerParams(vmem_limit_bytes=GRANT),
        name="pack",
    )(place, key_states, value_states, cosine, sine)


def turn_kernel(queries, cosine, sine, out):
    for head in range(queries.shape[1] // HD):
        part = (slice(None), slice(head * HD, (head + 1) * HD))
        out[part] = rotate(queries[part], cosine[...], sine[...])


def turn(queries, cosine, sine):
    return pl.pallas_call(
        turn_kernel,
        in_specs=[VMEM] * 3,
        out_specs=VMEM,
        out_shape=jax.ShapeDtypeStruct(queries.shape, jnp.bfloat16),
        compiler_params=pltpu.CompilerParams(vmem_limit_bytes=GRANT),
        name="turn",
    )(queries, cosine, sine)


def attended(table, head, verticals, slashes, block, rot, keys, values, causal):
    at = head * (verticals + slashes)
    verts = [table[at + i] for i in range(verticals)]
    slots = [(block, None)] + [(v, v < block) for v in verts]
    for j in range(1, slashes):
        u = block - table[at + verticals + j]
        valid = u >= 0
        for v in verts:
            valid = jnp.logical_and(valid, u != v)
        slots.append((jnp.maximum(u, 0), valid))
    rows = [pl.ds(pl.multiple_of(u * BLK, BLK), BLK) for u, _ in slots]
    pairs = [slice(i, i + 2) for i in range(0, len(slots), 2)]
    scores = []
    for pair in pairs:
        tile = jnp.concatenate([keys[r, :] for r in rows[pair]], axis=0)
        both = lax.dot_general(
            rot, tile, (((1,), (1,)), ((), ())), preferred_element_type=jnp.float32
        )
        for i, (_, valid) in enumerate(slots[pair]):
            s = both[:, i * BLK : (i + 1) * BLK]
            scores.append(
                jnp.where(causal, s, NEG) if valid is None else s + jnp.where(valid, 0.0, NEG)
            )
    top = jnp.max(functools.reduce(jnp.maximum, scores), axis=1, keepdims=True)
    weights = [jnp.exp2((s - top) * SCALE).astype(jnp.bfloat16) for s in scores]
    total = None
    for pair in pairs:
        tile = jnp.concatenate([values[r, :] for r in rows[pair]], axis=0)
        part = jnp.dot(
            jnp.concatenate(weights[pair], axis=1), tile, preferred_element_type=jnp.float32
        )
        total = part if total is None else total + part
    return (total[:, :HD] / total[:, HD:]).astype(jnp.bfloat16)


def attention_kernel(shape, table, queries, own, other, *refs):
    verticals, slashes, at, step = shape
    *outs, keys, values = refs
    ctx, core = table[at], table[at + 1]

    @pl.when(pl.program_id(0) == 0)
    def _():
        for d in range(own.shape[0] // BLK):
            for ref, parity in ((own, core), (other, 1 - core)):
                rows = pl.ds(pl.multiple_of(((ctx ^ d) * 2 + parity) * BLK, BLK), BLK)
                keys[rows, :] = ref[d * BLK : (d + 1) * BLK, :HD]
                values[rows, :HD] = ref[d * BLK : (d + 1) * BLK, HD:]
        values[:, HD:] = jnp.ones((values.shape[0], HD), values.dtype)

    causal = lax.broadcasted_iota(jnp.int32, (BLK, BLK), 1) <= lax.broadcasted_iota(
        jnp.int32, (BLK, BLK), 0
    )
    for i in range(step):
        head = pl.program_id(0) * step + i
        lanes = slice(i * HD, (i + 1) * HD)
        for local, out in enumerate(outs):
            rot = queries[local * BLK : (local + 1) * BLK, lanes]
            index = ctx * len(outs) + local
            out[:, lanes] = attended(
                table, head, verticals, slashes, index, rot, keys, values, causal
            )


def attend(table, at, verticals, slashes, queries, own, other):
    tokens, width = queries.shape
    step = 4
    whole = lambda a: pl.BlockSpec(a.shape, lambda h, _: (0, 0))
    part = lambda rows: pl.BlockSpec((rows, step * HD), lambda h, _: (0, h))
    blocks = tokens // BLK
    keys = 2 * own.shape[0]
    return pl.pallas_call(
        functools.partial(attention_kernel, (verticals, slashes, at, step)),
        grid_spec=pltpu.PrefetchScalarGridSpec(
            num_scalar_prefetch=1,
            grid=(width // (step * HD),),
            in_specs=[part(tokens), whole(own), whole(other)],
            out_specs=[part(BLK)] * blocks,
            scratch_shapes=[
                pltpu.VMEM((keys, HD), jnp.bfloat16),
                pltpu.VMEM((keys, 2 * HD), jnp.bfloat16),
            ],
        ),
        out_shape=[jax.ShapeDtypeStruct((BLK, width), jnp.bfloat16)] * blocks,
        compiler_params=pltpu.CompilerParams(vmem_limit_bytes=GRANT),
        name="attention",
    )(table, queries, own, other)


def hold_kernel(own, other, own_out, other_out, semaphores):
    copies = [
        pltpu.make_async_copy(source, target, semaphores.at[i])
        for i, (source, target) in enumerate(((own, own_out), (other, other_out)))
    ]
    for copy in copies:
        copy.start()
    for copy in copies:
        copy.wait()


def hold(own, other):
    return pl.pallas_call(
        hold_kernel,
        in_specs=[pl.BlockSpec(memory_space=pl.ANY)] * 2,
        out_specs=[VMEM] * 2,
        out_shape=[pltpu.VMEM(own.shape, own.dtype), pltpu.VMEM(other.shape, other.dtype)],
        scratch_shapes=[pltpu.SemaphoreType.DMA((2,))],
        compiler_params=pltpu.CompilerParams(vmem_limit_bytes=GRANT),
        name="hold",
    )(own, other)


def project_kernel(rows, own, other, out):
    depth, tile = own.shape[0], 512
    first, second = rows[:, :depth], rows[:, depth:]
    for j in range(0, own.shape[1], tile):
        part = slice(j, j + tile)
        total = jnp.dot(first, own[:, part], preferred_element_type=jnp.float32)
        total += jnp.dot(second, other[:, part], preferred_element_type=jnp.float32)
        out[:, part] = total.astype(out.dtype)


def project(rows, own, other, kind):
    count, depth = rows.shape
    width = own.shape[1]
    return pl.pallas_call(
        project_kernel,
        in_specs=[VMEM] * 3,
        out_specs=VMEM,
        out_shape=jax.ShapeDtypeStruct((count, width), kind),
        compiler_params=pltpu.CompilerParams(vmem_limit_bytes=GRANT),
        cost_estimate=pl.CostEstimate(
            flops=2 * count * depth * width,
            bytes_accessed=2 * (count * depth + count * width),
            transcendentals=0,
        ),
        name="project",
    )(rows, own, other)


def route(table):
    pairs = []
    for y in range(2):
        for x in range(2):
            for (z, c), (z2, c2) in table.items():
                if x == 1:
                    z, c, z2, c2 = 3 - z, 1 - c, 3 - z2, 1 - c2
                pairs.append((((z * 2 + y) * 2 + x) * 2 + c, ((z2 * 2 + y) * 2 + x) * 2 + c2))
    return sorted(pairs)


HOP_1 = {(2, 0): (1, 0), (3, 1): (2, 1), (0, 0): (2, 0), (1, 1): (0, 1)}
HOP_2 = {(3, 1): (1, 1), (2, 0): (3, 0), (1, 1): (2, 1), (0, 0): (1, 0)}
HOP_3 = {(1, 0): (0, 0), (1, 1): (0, 1), (2, 0): (3, 0), (2, 1): (3, 1)}


def routed(order, halves, out_weight, ctx_index, head_index):
    both = ("ctx", "head")
    z, y, x, core = ctx_index // 2, ctx_index % 2, head_index // 2, head_index % 2
    far = jnp.where(x == 0, z, 3 - z)
    lane = jnp.where(x == 0, core, 1 - core)
    swap_core = [(i, i ^ 1) for i in range(4)]
    swap_x = [(i, i ^ 2) for i in range(4)]
    swap_y = [(i, i ^ 1) for i in range(8)]
    home, inner, first = z % 2 == core, (far == 1) | (far == 2), far >= 2
    count = len(halves)

    hops, sent, kept, parts, come = [], [], [], [], []
    for i, half in enumerate(halves):
        half = order.get(f"half_{i}", half)
        block = jnp.concatenate([half, lax.ppermute(half, "head", swap_core)], axis=1)
        order.put(f"block_{i}", block)
        block = order.get(f"block_{i}", block)
        hop_1 = lax.ppermute(block, both, route(HOP_1))
        hop_2 = lax.ppermute(block, both, route(HOP_2))
        order.put(f"hop_1_{i}", hop_1)
        order.put(f"hop_2_{i}", hop_2)
        hops.append((block, hop_1, hop_2))
    other = lax.ppermute(order.get("weight", out_weight), "head", swap_core)
    weights = [out_weight, order.put("weight", other)]
    weights = hold(*order.get("hold", weights))
    order.put("weights", weights)

    def partial(rows, slot):
        part = project(order.get(f"sent_{slot}", rows), *weights, jnp.bfloat16)
        order.put(f"part_{slot}", part)
        out = order.get(f"part_out_{slot}", part)
        come.append(order.put(f"come_{slot}", lax.ppermute(out, "head", swap_x)))

    for i, (block, hop_1, hop_2) in enumerate(hops):
        passed = order.get(f"pass_{i}", jnp.where(lane == 0, hop_1, hop_2))
        hop_3 = order.put(f"hop_3_{i}", lax.ppermute(passed, both, route(HOP_3)))
        hop_3 = order.get(f"hop_3_out_{i}", hop_3)
        early = jnp.where(home, block, jnp.where(lane == 0, hop_2, hop_1))
        late = jnp.where(inner, passed, hop_3)
        sent.append(order.put(f"rows_{i}", jnp.where(first, early, late)))
        kept.append(order.put(f"kept_{i}", jnp.where(first, late, early)))
        partial(sent[i], i)
    sent_y, kept_y = [], []
    for i, rows in enumerate(sent):
        out = order.get(f"sent_out_{i}", rows)
        sent_y.append(order.put(f"sent_y_{i}", lax.ppermute(out, "ctx", swap_y)))
    for i, rows in enumerate(kept):
        out = order.get(f"kept_out_{i}", rows)
        kept_y.append(order.put(f"kept_y_{i}", lax.ppermute(out, "ctx", swap_y)))
    for i, rows in enumerate(sent_y):
        partial(rows, count + i)
    own = []
    for i, rows in enumerate((kept, kept_y)):
        rows = order.get(f"own_{i}", jnp.concatenate(rows, axis=0))
        own.append(order.put(f"own_done_{i}", project(rows, *weights, jnp.float32)))
    out = jnp.zeros((2 * count * BLK, out_weight.shape[1]), jnp.bfloat16)
    for i, theirs in enumerate(come):
        local, other_y = i % count, i // count
        mine = own[other_y][local * BLK : (local + 1) * BLK]
        total = (mine + theirs.astype(jnp.float32)).astype(jnp.bfloat16)
        at = (jnp.where(other_y == 0, y, 1 - y) * count + local) * BLK
        out = lax.dynamic_update_slice(out, total, (at, 0))
    return out


def collected(head_out, out_weight):
    rows = lax.all_gather(head_out, "ctx", axis=0, tiled=True)
    partial_terms = jnp.dot(rows, out_weight, preferred_element_type=jnp.float32)
    return lax.psum_scatter(
        partial_terms.astype(jnp.bfloat16), "head", scatter_dimension=0, tiled=True
    )


def per_device(
    ctx_size,
    head_size,
    queries,
    key_states,
    value_states,
    vertical_blocks,
    slash_offsets,
    positions,
    out_weight,
):
    local_heads = queries.shape[1] // HD
    head_index = lax.axis_index("head")
    ctx_index = lax.axis_index("ctx")
    core = head_index % 2
    shared_head = head_index * local_heads // GROUP
    counts = (vertical_blocks.shape[1], slash_offsets.shape[1])
    swap_core = [(i, i ^ 1) for i in range(head_size)]
    table = jnp.concatenate([vertical_blocks, slash_offsets], axis=1).reshape(-1)
    at = table.shape[0]
    table = jnp.concatenate([table, jnp.stack([ctx_index, core])])
    cosine, sine = rotation_tables(positions)
    piece = pack(jnp.stack([core, shared_head]), key_states, value_states, cosine, sine)
    pieces = [piece] + [
        lax.ppermute(piece, "ctx", [(i, i ^ d) for i in range(ctx_size)])
        for d in range(1, ctx_size)
    ]
    rotated = turn(queries, cosine, sine)
    own, rotated, table = lax.optimization_barrier(
        (jnp.concatenate(pieces, axis=0), rotated, table)
    )
    other = lax.ppermute(own, "head", swap_core)
    halves = attend(table, at, *counts, rotated, own, other)
    if (ctx_size, head_size) == (8, 4):
        return routed(Ordered(), halves, out_weight, ctx_index, head_index)
    return collected(jnp.concatenate(halves, axis=0), out_weight)


def solution(mesh):
    placed = (
        P("ctx", "head"),
        P("ctx", None),
        P("ctx", None),
        P("head", None),
        P("head", None),
        P("ctx"),
        P("head", "ctx"),
    )
    return jax.shard_map(
        functools.partial(per_device, mesh.shape["ctx"], mesh.shape["head"]),
        mesh=mesh,
        in_specs=placed,
        out_specs=P("head", "ctx"),
        check_vma=False,
    )
```

```python
import functools
import math

import jax
import jax.numpy as jnp
from jax import lax
from jax.experimental import pallas as pl
from jax.experimental.pallas import tpu as pltpu
from jax.sharding import PartitionSpec as P

HD = 128
GROUP = 16
BLK = 128
NEG = -1e30
GRANT = 20 << 20
BEFORE = {'hop_3_out_1': ('part_0',),
 'kept_out_0': ('part_0',),
 'kept_out_1': ('part_2',),
 'own_0': ('part_3',),
 'own_1': ('own_done_0',),
 'sent_2': ('come_0', 'part_1'),
 'sent_3': ('come_1', 'part_2'),
 'sent_out_1': ('sent_y_0',)}
SCALE = math.log2(math.e) / math.sqrt(HD)
VMEM = pl.BlockSpec(memory_space=pltpu.VMEM)
SMEM = pl.BlockSpec(memory_space=pltpu.SMEM)


class Ordered:
    def __init__(self):
        self.made = {}

    def put(self, name, value):
        self.made[name] = value
        return value

    def get(self, name, value):
        others = [self.made[other] for other in BEFORE.get(name, ()) if other in self.made]
        return lax.optimization_barrier((value, others))[0] if others else value


def rotation_tables(positions):
    half = HD // 2
    exponents = jnp.arange(half, dtype=jnp.float32) * (2.0 / HD)
    inverse_freq = 500000.0 ** (-exponents)
    angles = positions.astype(jnp.float32)[:, None] * inverse_freq[None, :]
    cosine, sine = jnp.cos(angles), jnp.sin(angles)
    return jnp.concatenate([cosine, cosine], axis=1), jnp.concatenate([-sine, sine], axis=1)


def rotate(states, cosine, sine):
    states = states.astype(jnp.float32)
    rotated = states * cosine + pltpu.roll(states, HD // 2, 1) * sine
    return rotated.astype(jnp.bfloat16)


def pack_kernel(place, keys, values, cosine, sine, piece):
    rows = pl.ds(pl.multiple_of(place[0] * BLK, BLK), BLK)
    lane = pl.ds(pl.multiple_of(place[1] * HD, HD), HD)
    piece[:, :HD] = rotate(keys[rows, lane], cosine[rows, :], sine[rows, :])
    piece[:, HD:] = values[rows, lane]


def pack(place, key_states, value_states, cosine, sine):
    return pl.pallas_call(
        pack_kernel,
        in_specs=[SMEM] + [VMEM] * 4,
        out_specs=VMEM,
        out_shape=jax.ShapeDtypeStruct((BLK, 2 * HD), jnp.bfloat16),
        compiler_params=pltpu.CompilerParams(vmem_limit_bytes=GRANT),
        name="pack",
    )(place, key_states, value_states, cosine, sine)


def turn_kernel(queries, cosine, sine, out):
    for head in range(queries.shape[1] // HD):
        part = (slice(None), slice(head * HD, (head + 1) * HD))
        out[part] = rotate(queries[part], cosine[...], sine[...])


def turn(queries, cosine, sine):
    return pl.pallas_call(
        turn_kernel,
        in_specs=[VMEM] * 3,
        out_specs=VMEM,
        out_shape=jax.ShapeDtypeStruct(queries.shape, jnp.bfloat16),
        compiler_params=pltpu.CompilerParams(vmem_limit_bytes=GRANT),
        name="turn",
    )(queries, cosine, sine)


def attended(table, head, verticals, slashes, block, rot, keys, values, causal):
    at = head * (verticals + slashes)
    verts = [table[at + i] for i in range(verticals)]
    slots = [(block, None)] + [(v, v < block) for v in verts]
    for j in range(1, slashes):
        u = block - table[at + verticals + j]
        valid = u >= 0
        for v in verts:
            valid = jnp.logical_and(valid, u != v)
        slots.append((jnp.maximum(u, 0), valid))
    rows = [pl.ds(pl.multiple_of(u * BLK, BLK), BLK) for u, _ in slots]
    pairs = [slice(i, i + 2) for i in range(0, len(slots), 2)]
    scores = []
    for pair in pairs:
        tile = jnp.concatenate([keys[r, :] for r in rows[pair]], axis=0)
        both = lax.dot_general(
            rot, tile, (((1,), (1,)), ((), ())), preferred_element_type=jnp.float32
        )
        for i, (_, valid) in enumerate(slots[pair]):
            s = both[:, i * BLK : (i + 1) * BLK]
            scores.append(
                jnp.where(causal, s, NEG) if valid is None else s + jnp.where(valid, 0.0, NEG)
            )
    top = jnp.max(functools.reduce(jnp.maximum, scores), axis=1, keepdims=True)
    weights = [jnp.exp2((s - top) * SCALE).astype(jnp.bfloat16) for s in scores]
    total = None
    for pair in pairs:
        tile = jnp.concatenate([values[r, :] for r in rows[pair]], axis=0)
        part = jnp.dot(
            jnp.concatenate(weights[pair], axis=1), tile, preferred_element_type=jnp.float32
        )
        total = part if total is None else total + part
    return (total[:, :HD] / total[:, HD:]).astype(jnp.bfloat16)


def attention_kernel(shape, table, queries, own, other, *refs):
    verticals, slashes, at, step = shape
    *outs, keys, values = refs
    ctx, core = table[at], table[at + 1]

    @pl.when(pl.program_id(0) == 0)
    def _():
        for d in range(own.shape[0] // BLK):
            for ref, parity in ((own, core), (other, 1 - core)):
                rows = pl.ds(pl.multiple_of(((ctx ^ d) * 2 + parity) * BLK, BLK), BLK)
                keys[rows, :] = ref[d * BLK : (d + 1) * BLK, :HD]
                values[rows, :HD] = ref[d * BLK : (d + 1) * BLK, HD:]
        values[:, HD:] = jnp.ones((values.shape[0], HD), values.dtype)

    causal = lax.broadcasted_iota(jnp.int32, (BLK, BLK), 1) <= lax.broadcasted_iota(
        jnp.int32, (BLK, BLK), 0
    )
    for i in range(step):
        head = pl.program_id(0) * step + i
        lanes = slice(i * HD, (i + 1) * HD)
        for local, out in enumerate(outs):
            rot = queries[local * BLK : (local + 1) * BLK, lanes]
            index = ctx * len(outs) + local
            out[:, lanes] = attended(
                table, head, verticals, slashes, index, rot, keys, values, causal
            )


def attend(table, at, verticals, slashes, queries, own, other):
    tokens, width = queries.shape
    step = 4
    whole = lambda a: pl.BlockSpec(a.shape, lambda h, _: (0, 0))
    part = lambda rows: pl.BlockSpec((rows, step * HD), lambda h, _: (0, h))
    blocks = tokens // BLK
    keys = 2 * own.shape[0]
    return pl.pallas_call(
        functools.partial(attention_kernel, (verticals, slashes, at, step)),
        grid_spec=pltpu.PrefetchScalarGridSpec(
            num_scalar_prefetch=1,
            grid=(width // (step * HD),),
            in_specs=[part(tokens), whole(own), whole(other)],
            out_specs=[part(BLK)] * blocks,
            scratch_shapes=[
                pltpu.VMEM((keys, HD), jnp.bfloat16),
                pltpu.VMEM((keys, 2 * HD), jnp.bfloat16),
            ],
        ),
        out_shape=[jax.ShapeDtypeStruct((BLK, width), jnp.bfloat16)] * blocks,
        compiler_params=pltpu.CompilerParams(vmem_limit_bytes=GRANT),
        name="attention",
    )(table, queries, own, other)


def hold_kernel(own, other, own_out, other_out, semaphores):
    copies = [
        pltpu.make_async_copy(source, target, semaphores.at[i])
        for i, (source, target) in enumerate(((own, own_out), (other, other_out)))
    ]
    for copy in copies:
        copy.start()
    for copy in copies:
        copy.wait()


def hold(own, other):
    return pl.pallas_call(
        hold_kernel,
        in_specs=[pl.BlockSpec(memory_space=pl.ANY)] * 2,
        out_specs=[VMEM] * 2,
        out_shape=[pltpu.VMEM(own.shape, own.dtype), pltpu.VMEM(other.shape, other.dtype)],
        scratch_shapes=[pltpu.SemaphoreType.DMA((2,))],
        compiler_params=pltpu.CompilerParams(vmem_limit_bytes=GRANT),
        name="hold",
    )(own, other)


def project_kernel(rows, own, other, out):
    depth, tile = own.shape[0], 512
    first, second = rows[:, :depth], rows[:, depth:]
    for j in range(0, own.shape[1], tile):
        part = slice(j, j + tile)
        total = jnp.dot(first, own[:, part], preferred_element_type=jnp.float32)
        total += jnp.dot(second, other[:, part], preferred_element_type=jnp.float32)
        out[:, part] = total.astype(out.dtype)


def project(rows, own, other, kind):
    count, depth = rows.shape
    width = own.shape[1]
    return pl.pallas_call(
        project_kernel,
        in_specs=[VMEM] * 3,
        out_specs=VMEM,
        out_shape=jax.ShapeDtypeStruct((count, width), kind),
        compiler_params=pltpu.CompilerParams(vmem_limit_bytes=GRANT),
        cost_estimate=pl.CostEstimate(
            flops=2 * count * depth * width,
            bytes_accessed=2 * (count * depth + count * width),
            transcendentals=0,
        ),
        name="project",
    )(rows, own, other)


def route(table):
    pairs = []
    for y in range(2):
        for x in range(2):
            for (z, c), (z2, c2) in table.items():
                if x == 1:
                    z, c, z2, c2 = 3 - z, 1 - c, 3 - z2, 1 - c2
                pairs.append((((z * 2 + y) * 2 + x) * 2 + c, ((z2 * 2 + y) * 2 + x) * 2 + c2))
    return sorted(pairs)


HOP_1 = {(2, 0): (1, 0), (3, 1): (2, 1), (0, 0): (2, 0), (1, 1): (0, 1)}
HOP_2 = {(3, 1): (1, 1), (2, 0): (3, 0), (1, 1): (2, 1), (0, 0): (1, 0)}
HOP_3 = {(1, 0): (0, 0), (1, 1): (0, 1), (2, 0): (3, 0), (2, 1): (3, 1)}


def routed(order, halves, out_weight, ctx_index, head_index):
    both = ("ctx", "head")
    z, y, x, core = ctx_index // 2, ctx_index % 2, head_index // 2, head_index % 2
    far = jnp.where(x == 0, z, 3 - z)
    lane = jnp.where(x == 0, core, 1 - core)
    swap_core = [(i, i ^ 1) for i in range(4)]
    swap_x = [(i, i ^ 2) for i in range(4)]
    swap_y = [(i, i ^ 1) for i in range(8)]
    home, inner, first = z % 2 == core, (far == 1) | (far == 2), far >= 2
    count = len(halves)

    hops, sent, kept, parts, come = [], [], [], [], []
    for i, half in enumerate(halves):
        half = order.get(f"half_{i}", half)
        block = jnp.concatenate([half, lax.ppermute(half, "head", swap_core)], axis=1)
        order.put(f"block_{i}", block)
        block = order.get(f"block_{i}", block)
        hop_1 = lax.ppermute(block, both, route(HOP_1))
        hop_2 = lax.ppermute(block, both, route(HOP_2))
        order.put(f"hop_1_{i}", hop_1)
        order.put(f"hop_2_{i}", hop_2)
        hops.append((block, hop_1, hop_2))
    other = lax.ppermute(order.get("weight", out_weight), "head", swap_core)
    weights = [out_weight, order.put("weight", other)]
    weights = hold(*order.get("hold", weights))
    order.put("weights", weights)

    def partial(rows, slot):
        part = project(order.get(f"sent_{slot}", rows), *weights, jnp.bfloat16)
        order.put(f"part_{slot}", part)
        out = order.get(f"part_out_{slot}", part)
        come.append(order.put(f"come_{slot}", lax.ppermute(out, "head", swap_x)))

    for i, (block, hop_1, hop_2) in enumerate(hops):
        passed = order.get(f"pass_{i}", jnp.where(lane == 0, hop_1, hop_2))
        hop_3 = order.put(f"hop_3_{i}", lax.ppermute(passed, both, route(HOP_3)))
        hop_3 = order.get(f"hop_3_out_{i}", hop_3)
        early = jnp.where(home, block, jnp.where(lane == 0, hop_2, hop_1))
        late = jnp.where(inner, passed, hop_3)
        sent.append(order.put(f"rows_{i}", jnp.where(first, early, late)))
        kept.append(order.put(f"kept_{i}", jnp.where(first, late, early)))
        partial(sent[i], i)
    sent_y, kept_y = [], []
    for i, rows in enumerate(sent):
        out = order.get(f"sent_out_{i}", rows)
        sent_y.append(order.put(f"sent_y_{i}", lax.ppermute(out, "ctx", swap_y)))
    for i, rows in enumerate(kept):
        out = order.get(f"kept_out_{i}", rows)
        kept_y.append(order.put(f"kept_y_{i}", lax.ppermute(out, "ctx", swap_y)))
    for i, rows in enumerate(sent_y):
        partial(rows, count + i)
    own = []
    for i, rows in enumerate((kept, kept_y)):
        rows = order.get(f"own_{i}", jnp.concatenate(rows, axis=0))
        own.append(order.put(f"own_done_{i}", project(rows, *weights, jnp.float32)))
    out = jnp.zeros((2 * count * BLK, out_weight.shape[1]), jnp.bfloat16)
    for i, theirs in enumerate(come):
        local, other_y = i % count, i // count
        mine = own[other_y][local * BLK : (local + 1) * BLK]
        total = (mine + theirs.astype(jnp.float32)).astype(jnp.bfloat16)
        at = (jnp.where(other_y == 0, y, 1 - y) * count + local) * BLK
        out = lax.dynamic_update_slice(out, total, (at, 0))
    return out


def collected(head_out, out_weight):
    rows = lax.all_gather(head_out, "ctx", axis=0, tiled=True)
    partial_terms = jnp.dot(rows, out_weight, preferred_element_type=jnp.float32)
    return lax.psum_scatter(
        partial_terms.astype(jnp.bfloat16), "head", scatter_dimension=0, tiled=True
    )


def per_device(
    ctx_size,
    head_size,
    queries,
    key_states,
    value_states,
    vertical_blocks,
    slash_offsets,
    positions,
    out_weight,
):
    local_heads = queries.shape[1] // HD
    head_index = lax.axis_index("head")
    ctx_index = lax.axis_index("ctx")
    core = head_index % 2
    shared_head = head_index * local_heads // GROUP
    counts = (vertical_blocks.shape[1], slash_offsets.shape[1])
    swap_core = [(i, i ^ 1) for i in range(head_size)]
    table = jnp.concatenate([vertical_blocks, slash_offsets], axis=1).reshape(-1)
    at = table.shape[0]
    table = jnp.concatenate([table, jnp.stack([ctx_index, core])])
    cosine, sine = rotation_tables(positions)
    piece = pack(jnp.stack([core, shared_head]), key_states, value_states, cosine, sine)
    pieces = [piece] + [
        lax.ppermute(piece, "ctx", [(i, i ^ d) for i in range(ctx_size)])
        for d in range(1, ctx_size)
    ]
    rotated = turn(queries, cosine, sine)
    own, rotated, table = lax.optimization_barrier(
        (jnp.concatenate(pieces, axis=0), rotated, table)
    )
    other = lax.ppermute(own, "head", swap_core)
    halves = attend(table, at, *counts, rotated, own, other)
    if (ctx_size, head_size) == (8, 4):
        return routed(Ordered(), halves, out_weight, ctx_index, head_index)
    return collected(jnp.concatenate(halves, axis=0), out_weight)


def solution(mesh):
    placed = (
        P("ctx", "head"),
        P("ctx", None),
        P("ctx", None),
        P("head", None),
        P("head", None),
        P("ctx"),
        P("head", "ctx"),
    )
    return jax.shard_map(
        functools.partial(per_device, mesh.shape["ctx"], mesh.shape["head"]),
        mesh=mesh,
        in_specs=placed,
        out_specs=P("head", "ctx"),
        check_vma=False,
    )
```
